32 devices in a mesh: blk: 16 (over z, x, core), ctx: 2 (over y).
Axes of the slice: x: 2, y: 2, z: 4, core: 2. Of those that a mesh axis runs over, the one named last changes fastest.
Arguments:
- inputs: bfloat16 [4096, 2048], P(('blk', 'ctx')), may hold values from -6 to 6
- out_grad: bfloat16 [4096, 2048], P(('blk', 'ctx')), may hold values from -6 to 6
- seq_lengths: int32 [16], replicated, may hold values from 1 to 1024, 4096 in all
- key_live: int32 [4096], replicated, may hold values 0 or 1
- attn_gain: bfloat16 [2048], P(('blk', 'ctx')), may hold values from 0.5 to 1.5
- q_down: bfloat16 [2048, 1024], P(('blk', 'ctx')), may hold values from -0.125 to 0.125
- q_gain: bfloat16 [1024], P(('blk', 'ctx')), may hold values from 0.5 to 1.5
- q_up: bfloat16 [1024, 4096], P(('blk', 'ctx')), may hold values from -0.1875 to 0.1875
- k_proj: bfloat16 [2048, 256], P(('blk', 'ctx')), may hold values from -0.125 to 0.125
- v_proj: bfloat16 [2048, 256], P(('blk', 'ctx')), may hold values from -0.125 to 0.125
- o_proj: bfloat16 [4096, 2048], P(('blk', 'ctx')), may hold values from -1.5 to 1.5
- ffn_gain: bfloat16 [2048], P(('blk', 'ctx')), may hold values from 0.5 to 1.5
- w_gate: bfloat16 [2048, 5632], P(('blk', 'ctx')), may hold values from -0.125 to 0.125
- w_up: bfloat16 [2048, 5632], P(('blk', 'ctx')), may hold values from -0.125 to 0.125
- w_down: bfloat16 [5632, 2048], P(('blk', 'ctx')), may hold values from -0.078125 to 0.078125
Outputs:
- output: bfloat16 [4096, 2048], P(('blk', 'ctx'))
- input_grad: float32 [4096, 2048], P(('blk', 'ctx'))
- attn_gain_grad: float32 [2048], P(('blk', 'ctx'))
- q_down_grad: float32 [2048, 1024], P(('blk', 'ctx'))
- q_gain_grad: float32 [1024], P(('blk', 'ctx'))
- q_up_grad: float32 [1024, 4096], P(('blk', 'ctx'))
- k_proj_grad: float32 [2048, 256], P(('blk', 'ctx'))
- v_proj_grad: float32 [2048, 256], P(('blk', 'ctx'))
- o_proj_grad: float32 [4096, 2048], P(('blk', 'ctx'))
- ffn_gain_grad: float32 [2048], P(('blk', 'ctx'))
- w_gate_grad: float32 [2048, 5632], P(('blk', 'ctx'))
- w_up_grad: float32 [2048, 5632], P(('blk', 'ctx'))
- w_down_grad: float32 [5632, 2048], P(('blk', 'ctx'))
The draws below stay inside these ranges and needn't reach their ends.
Inputs may be any that keep to these rules, and one draw needn't show every extreme that they name: `seq_lengths`: 16 sequences packed in order, heavy-tailed lengths summing to 4096; the longest is exactly 1024.
All inputs are finite; a program needn't handle non-finite values.
Results may differ from the reference program's by a relative error of at most 0.015.
Values may be sent and summed in bfloat16 or wider, within the bound.
No kernel may reach another device: no remote copies, remote signals or barrier semaphores. Data moves between devices by JAX's collectives and lax.ppermute only.
A program may use at most 448 MiB of HBM per device.

```python
import math
import jax
import jax.numpy as jnp
import numpy as np
from jax import lax

D = 2048
QR = 1024
H = 16
HD = 256
FF = 5632
BLKTOK = 256
MAXLEN = 1024
TOKENS = 4096
NSEQ = 16


def set_ends(values, own_key, smallest, high):
    shape = values.shape
    index_at = [jax.random.randint(jax.random.fold_in(own_key, axis), (), 0, shape[axis]) for axis in range(len(shape))]
    values = values.at[tuple(index_at)].set(smallest)
    longest = shape.index(max(shape))
    index_at[longest] = (index_at[longest] + 1) % shape[longest]
    return values.at[tuple(index_at)].set(high)


def levels(stream_key, dims, shards, least, largest):
    def one(dim, blocks):
        steps = jax.random.uniform(jax.random.fold_in(jax.random.fold_in(stream_key, 6), dim), (blocks,), jnp.float32, least / len(shards), largest / len(shards))
        return jnp.repeat(jnp.exp(steps), dims[dim] // blocks).reshape((-1,) + (1,) * (len(dims) - dim - 1))

    loudness = one(*shards[0])
    for cut in shards[1:]:
        loudness = loudness * one(*cut)
    return loudness


def profile(amount, total, reach, lean):
    weights = [(1 << 20) // math.isqrt(standing ** lean) + 1 for standing in range(2, amount + 1)]
    spare, given = total - reach - (amount - 1), [1] * (amount - 1)
    while spare > 0:
        movable = [i for i in range(amount - 1) if given[i] < reach]
        pool, remaining = sum([weights[i] for i in movable]), spare
        for i in movable:
            more = min(reach - given[i], max(1, remaining * weights[i] // pool), spare)
            given[i] = given[i] + more
            spare = spare - more
    return np.array([reach] + given)


def uneven(rng, count, total, bound, lean):
    if count == 2:
        one = jax.random.randint(rng, (), max(1, total - bound), min(bound, total - 1) + 1)
        return jnp.stack([one, total - one])
    sizes = jnp.asarray(profile(count, total, bound, lean), jnp.int32)
    twos = (count - 1) // 2
    donor, taker = sizes[1:1 + 2 * twos:2], sizes[2:2 + 2 * twos:2]
    room = jnp.minimum(donor - 1, bound - taker)
    moved = jax.random.randint(jax.random.fold_in(rng, 1), (twos,), 0, 1 << 20) % (room + 1)
    sizes = sizes.at[1:1 + 2 * twos:2].set(donor - moved).at[2:2 + 2 * twos:2].set(taker + moved)
    return sizes[jax.random.permutation(jax.random.fold_in(rng, 2), count)]


def centred(stream_key, dims, width, most, split=(), kind=jnp.bfloat16):
    entries = jax.random.normal(stream_key, dims, jnp.float32) * width
    if len(split) > 0:
        entries = levels(stream_key, dims, split, -0.22, 0.18) * entries
    return jnp.clip(entries, min=-most, max=most).astype(kind)


def setup_inputs(seed: int = 0) -> dict:
    keys = jax.random.split(jax.random.key(seed), 16)
    return {
        "inputs": centred(keys[0], (TOKENS, D), 1.0, 6.0, ((0, 32),)),
        "out_grad": centred(keys[1], (TOKENS, D), 1.0, 6.0, ((0, 32),)),
        "seq_lengths": uneven(keys[2], NSEQ, TOKENS, MAXLEN, 2).astype(jnp.int32),
        "key_live": set_ends((jax.random.randint(keys[3], (TOKENS,), 0, 8) < 7).astype(jnp.int32), jax.random.fold_in(keys[3], 1), 0, 1),
        "attn_gain": jnp.clip(1.0 + 0.1 * jax.random.normal(keys[4], (D,), jnp.float32), 0.5, 1.5).astype(jnp.bfloat16),
        "q_down": centred(keys[5], (D, QR), D ** -0.5, 0.125, ((0, 32),)),
        "q_gain": jnp.clip(1.0 + 0.1 * jax.random.normal(keys[6], (QR,), jnp.float32), 0.5, 1.5).astype(jnp.bfloat16),
        "q_up": centred(keys[7], (QR, H * HD), QR ** -0.5, 0.1875, ((0, 32),)),
        "k_proj": centred(keys[8], (D, HD), D ** -0.5, 0.125, ((0, 32),)),
        "v_proj": centred(keys[9], (D, HD), D ** -0.5, 0.125, ((0, 32),)),
        "o_proj": centred(keys[10], (H * HD, D), (max(4, H * HD // 256)) ** -0.5, 1.5, ((0, 32),)),
        "ffn_gain": jnp.clip(1.0 + 0.1 * jax.random.normal(keys[11], (D,), jnp.float32), 0.5, 1.5).astype(jnp.bfloat16),
        "w_gate": centred(keys[12], (D, FF), D ** -0.5, 0.125, ((0, 32),)),
        "w_up": centred(keys[13], (D, FF), D ** -0.5, 0.125, ((0, 32),)),
        "w_down": centred(keys[14], (FF, D), FF ** -0.5, 0.078125, ((0, 32),)),
    }


@jax.custom_vjp
def low(v):
    return lax.optimization_barrier(v.astype(jnp.bfloat16)).astype(jnp.float32)

@jax.custom_vjp
def low_back(v):
    return v

def low_keep(v):
    return (low(v), None)

def low_pass(kept, grad):
    return (grad,)

def back_keep(v):
    return (v, None)

def back_low(kept, grad):
    return (low(grad),)
low.defvjp(low_keep, low_pass)
low_back.defvjp(back_keep, back_low)
EPSILON = 1e-06
ROPE_BASE = 10000.0
NEGATIVE = -1e+30
EXACT = lax.Precision.HIGHEST

def token_tables(seq_lengths, token_index):
    seq_ends = jnp.cumsum(seq_lengths).astype(jnp.int32)
    passed = seq_ends[None, :] <= token_index[:, None]
    segment = lax.optimization_barrier(jnp.sum(passed.astype(jnp.int32), axis=1)).astype(jnp.int32)
    seq_start = lax.optimization_barrier(jnp.sum(jnp.where(passed, seq_lengths[None, :], 0), axis=1)).astype(jnp.int32)
    return (segment, token_index - seq_start)

def rope_tables(position, head_width):
    half_width = head_width // 2
    frequency = ROPE_BASE ** (-(2.0 * jnp.arange(half_width, dtype=jnp.float32)) / head_width)
    angles = position.astype(jnp.float32)[:, None] * frequency[None, :]
    return (jnp.cos(angles), jnp.sin(angles))

def rotate(source, cosines, sines):
    half_width = source.shape[-1] // 2
    first = source[..., :half_width]
    second = source[..., half_width:]
    return jnp.concatenate([first * cosines - second * sines, second * cosines + first * sines], axis=-1)

def norm(source, gain_row):
    return source * lax.rsqrt(lax.optimization_barrier(jnp.mean(source * source, axis=-1, keepdims=True)) + EPSILON) * gain_row

def matmul(left, right):
    return jnp.dot(left, right, precision=EXACT)

def attention(queries, key_rows, values, segment, key_live):
    block_count = queries.shape[0] // BLKTOK
    key_span = MAXLEN + BLKTOK
    scale = HD ** (-0.5)
    pad_keys = jnp.concatenate([jnp.zeros((MAXLEN, HD), jnp.float32), key_rows], axis=0)
    pad_values = jnp.concatenate([jnp.zeros((MAXLEN, HD), jnp.float32), values], axis=0)

    def one_block(number):
        first = number * BLKTOK
        q_part = lax.dynamic_slice_in_dim(queries, first, BLKTOK, 0)
        k_part = lax.dynamic_slice_in_dim(pad_keys, first, key_span, 0)
        v_part = lax.dynamic_slice_in_dim(pad_values, first, key_span, 0)
        q_index = first + jnp.arange(BLKTOK, dtype=jnp.int32)
        k_index = first - MAXLEN + jnp.arange(key_span, dtype=jnp.int32)
        k_clip = jnp.maximum(k_index, 0).astype(jnp.int32)
        q_seg = lax.dynamic_slice_in_dim(segment, first, BLKTOK, 0)
        k_seg = jnp.take(segment, k_clip)
        k_live = jnp.take(key_live, k_clip)
        visible = (k_seg[None, :] == q_seg[:, None]) & (k_index[None, :] <= q_index[:, None])
        visible = visible & ((k_live[None, :] == 1) | (k_index[None, :] == q_index[:, None]))
        visible = visible & (k_index[None, :] >= 0)
        scores = low_back(jnp.einsum('thd,kd->thk', q_part, k_part, precision=EXACT) * scale)
        scores = jnp.where(visible[:, None, :], scores, NEGATIVE)
        row_max = lax.optimization_barrier(jnp.max(scores, axis=-1, keepdims=True))
        exp_scores = jnp.exp(scores - row_max)
        prob_low = low(exp_scores / lax.optimization_barrier(jnp.sum(exp_scores, axis=-1, keepdims=True)))
        return jnp.einsum('thk,kd->thd', prob_low, v_part, precision=EXACT)
    blocks_out = lax.map(jax.checkpoint(one_block), jnp.arange(block_count, dtype=jnp.int32))
    return blocks_out.reshape(queries.shape)

def forward_layer(inputs, attn_gain, q_down, q_gain, q_up, k_proj, v_proj, o_proj, ffn_gain, w_gate, w_up, w_down, cosines, sines, segment, key_live):
    rows_all = inputs.shape[0]
    normed = low(norm(inputs, attn_gain))
    latent = low_back(matmul(normed, q_down))
    latent_low = low(norm(latent, q_gain))
    q_pre = low_back(matmul(latent_low, q_up)).reshape(rows_all, H, HD)
    queries = low(rotate(q_pre, cosines[:, None, :], sines[:, None, :]))
    key_rows = low(rotate(low_back(matmul(normed, k_proj)), cosines, sines))
    values = low(low_back(matmul(normed, v_proj)))
    attended = attention(queries, key_rows, values, segment, key_live)
    attended = low_back(low(attended.reshape(rows_all, H * HD)))
    middle = inputs + low_back(matmul(attended, o_proj))
    normed_mid = low(norm(middle, ffn_gain))
    gate_act = low_back(matmul(normed_mid, w_gate))
    up_act = low_back(matmul(normed_mid, w_up))
    hidden = low(jax.nn.silu(gate_act) * up_act)
    return middle + matmul(hidden, w_down)

def reference(inputs, out_grad, seq_lengths, key_live, attn_gain, q_down, q_gain, q_up, k_proj, v_proj, o_proj, ffn_gain, w_gate, w_up, w_down):
    segment, position = token_tables(seq_lengths, jnp.arange(TOKENS, dtype=jnp.int32))
    cosines, sines = rope_tables(position, HD)
    leaves = tuple((operand.astype(jnp.float32) for operand in (inputs, attn_gain, q_down, q_gain, q_up, k_proj, v_proj, o_proj, ffn_gain, w_gate, w_up, w_down)))

    def forward_tuple(params):
        return forward_layer(*params, cosines, sines, segment, key_live)
    result, pullback = jax.vjp(forward_tuple, leaves)
    grads, = pullback(out_grad.astype(jnp.float32))
    return (result.astype(jnp.bfloat16), grads[0], grads[1], grads[2], grads[3], grads[4], grads[5], grads[6], grads[7], grads[8], grads[9], grads[10], grads[11])
```

```python
import jax
import jax.numpy as jnp
from jax import lax
from jax.experimental import pallas as pl
from jax.experimental.pallas import tpu as pltpu
from jax.sharding import Mesh
from jax.sharding import PartitionSpec as P

H = 16
HD = 256
HALF = HD // 2
EPSILON = 1e-06
ROPE_BASE = 10000.0
NEGATIVE = -1e30
LOW = jnp.bfloat16
WIDE = jnp.float32
TILE = 256

ALL = ("r", "x", "c", "y")
PLANE = ("x", "c", "y")


def token_tables(seq_lengths, token_index):
    seq_ends = jnp.cumsum(seq_lengths)
    passed = seq_ends[None, :] <= token_index[:, None]
    return jnp.sum(jnp.where(passed, seq_lengths[None, :], 0), axis=1)


def rope_tables(position):
    frequency = ROPE_BASE ** (-(2.0 * jnp.arange(HALF, dtype=WIDE)) / HD)
    angles = position.astype(WIDE)[:, None] * frequency[None, :]
    return (jnp.cos(angles), jnp.sin(angles))


def rotate(source, cosines, sines):
    first = source[..., :HALF]
    second = source[..., HALF:]
    return jnp.concatenate(
        [first * cosines - second * sines, second * cosines + first * sines], axis=-1
    )


def norm_forward(source, gain_row):
    inv_rms = lax.rsqrt(jnp.mean(source * source, axis=-1, keepdims=True) + EPSILON)
    return (source * inv_rms * gain_row, inv_rms)


def norm_backward(source, inv_rms, gain_row, cotangent):
    weighted = cotangent * gain_row
    d_source = inv_rms * weighted - source * inv_rms**3 * jnp.mean(
        weighted * source, axis=-1, keepdims=True
    )
    d_gain = jnp.sum(cotangent * source * inv_rms, axis=0)
    return (d_source, d_gain)


def dot(left, right, contract):
    return lax.dot_general(left, right, (contract, ((), ())), preferred_element_type=WIDE)


NN = ((1,), (0,))
NT = ((1,), (1,))
TN = ((0,), (0,))


def pick(array, index, axis=0):
    return lax.dynamic_index_in_dim(array, index, axis, keepdims=False)


def across(value, axis, mask):
    count = lax.axis_size(axis)
    return lax.ppermute(value, axis, [(source, source ^ mask) for source in range(count)])


def gathered(value, axes):
    blocks = [value] + [across(value, axes, mask) for mask in range(1, lax.axis_size(axes))]
    return blocks + [across(block, "c", 1) for block in blocks]


def reduced(mine, partners, axes):
    totals = mine + across(partners, "c", 1).astype(WIDE)
    result = totals[0]
    for mask in range(1, totals.shape[0]):
        result = result + across(totals[mask].astype(LOW), axes, mask).astype(WIDE)
    return result


def summed_over(parts, index, axes):
    result = pick(parts, index)
    for mask in range(1, lax.axis_size(axes)):
        sent = pick(parts, index ^ mask).astype(LOW)
        result = result + across(sent, axes, mask).astype(WIDE)
    return result


def visible_of(q_index, q_start, k_index, k_live):
    return ((k_live >= q_start) & (k_live <= q_index)) | (k_index == q_index)


def twice(value):
    return jnp.concatenate([value, value], axis=0)


def stacked(ref):
    return jnp.concatenate([ref[:, :HD], ref[:, HD:]], axis=0)


def attend_kernel(
    count, ids, q_ref, k_ref, v_ref, qi_ref, qs_ref, ki_ref, kl_ref, o_ref, lse_ref, s_ref, acc_ref
):
    step = pl.program_id(0)
    tiles = k_ref.shape[0] // TILE
    total = count[step]
    queries = stacked(q_ref)
    q_index, q_start = twice(qi_ref[...]), twice(qs_ref[...])

    def score(turn, row_max):
        tile = ids[step * tiles + turn]
        keys = k_ref[pl.ds(pl.multiple_of(tile * TILE, TILE), TILE), :]
        seen = visible_of(q_index, q_start, ki_ref[tile], kl_ref[tile])
        scores = jnp.where(seen, dot(queries, keys, NT) * (HD**-0.5), NEGATIVE)
        s_ref[turn] = scores
        return jnp.maximum(row_max, jnp.max(scores, axis=1, keepdims=True))

    row_max = lax.fori_loop(0, total, score, jnp.full((2 * TILE, 1), NEGATIVE, WIDE))
    acc_ref[...] = jnp.zeros_like(acc_ref)

    def attend(turn, denominator):
        tile = ids[step * tiles + turn]
        probs = jnp.exp(s_ref[turn] - row_max)
        values = v_ref[pl.ds(pl.multiple_of(tile * TILE, TILE), TILE), :]
        acc_ref[...] += dot(probs.astype(LOW), values, NN)
        return denominator + jnp.sum(probs, axis=1, keepdims=True)

    denominator = lax.fori_loop(0, total, attend, jnp.zeros((2 * TILE, 1), WIDE))
    result = (acc_ref[...] / denominator).astype(LOW)
    log_total = row_max + jnp.log(denominator)
    for head in range(2):
        rows = slice(head * TILE, (head + 1) * TILE)
        o_ref[:, head * HD : (head + 1) * HD] = result[rows]
        lse_ref[:, head : head + 1] = log_total[rows]


def attend_back_kernel(
    count,
    ids,
    q_ref,
    k_ref,
    v_ref,
    qi_ref,
    qs_ref,
    ki_ref,
    kl_ref,
    o_ref,
    do_ref,
    lse_ref,
    cos_ref,
    sin_ref,
    dq_ref,
    dk_ref,
    dv_ref,
    acc_ref,
):
    step = pl.program_id(0)
    tiles = k_ref.shape[0] // TILE

    @pl.when(step == 0)
    def _():
        dk_ref[...] = jnp.zeros_like(dk_ref)
        dv_ref[...] = jnp.zeros_like(dv_ref)

    queries, d_out = stacked(q_ref), stacked(do_ref)
    q_index, q_start = twice(qi_ref[...]), twice(qs_ref[...])
    log_total = jnp.concatenate([lse_ref[:, 0:1], lse_ref[:, 1:2]], axis=0)
    delta = jnp.sum(d_out.astype(WIDE) * stacked(o_ref).astype(WIDE), axis=1, keepdims=True)
    acc_ref[...] = jnp.zeros_like(acc_ref)
    scale = HD**-0.5

    def back(turn, unused):
        tile = ids[step * tiles + turn]
        rows = pl.ds(pl.multiple_of(tile * TILE, TILE), TILE)
        keys, values = k_ref[rows, :], v_ref[rows, :]
        seen = visible_of(q_index, q_start, ki_ref[tile], kl_ref[tile])
        scores = jnp.where(seen, dot(queries, keys, NT) * scale, NEGATIVE)
        soft = jnp.exp(scores - log_total)
        d_probs = dot(d_out, values, NT)
        d_scores = (soft * (d_probs - delta)).astype(LOW)
        dv_ref[rows, :] += dot(soft.astype(LOW), d_out, TN)
        dk_ref[rows, :] += dot(d_scores, queries, TN) * scale
        acc_ref[...] += dot(d_scores, keys, NN)
        return unused

    lax.fori_loop(0, count[step], back, 0)
    cosines, sines = cos_ref[...], sin_ref[...]
    for head in range(2):
        d_query = acc_ref[head * TILE : (head + 1) * TILE, :] * scale
        turned = rotate(d_query, cosines, -sines)
        dq_ref[:, head * HD : (head + 1) * HD] = turned.astype(LOW)


def by_query(width):
    return pl.BlockSpec((TILE, width), lambda i, *unused: (i, 0))


def whole(shape):
    return pl.BlockSpec(shape, lambda i, *unused: (0,) * len(shape))


def attend(count, ids, queries, keys, values, q_index, q_start, k_index, k_live):
    rows, span = queries.shape[0], keys.shape[0]
    tiles = span // TILE
    return pl.pallas_call(
        attend_kernel,
        grid_spec=pltpu.PrefetchScalarGridSpec(
            num_scalar_prefetch=2,
            grid=(rows // TILE,),
            in_specs=[
                by_query(2 * HD),
                whole((span, HD)),
                whole((span, HD)),
                by_query(1),
                by_query(1),
                whole((tiles, 1, TILE)),
                whole((tiles, 1, TILE)),
            ],
            out_specs=[by_query(2 * HD), by_query(2)],
            scratch_shapes=[
                pltpu.VMEM((tiles, 2 * TILE, TILE), WIDE),
                pltpu.VMEM((2 * TILE, HD), WIDE),
            ],
        ),
        out_shape=[
            jax.ShapeDtypeStruct((rows, 2 * HD), LOW),
            jax.ShapeDtypeStruct((rows, 2), WIDE),
        ],
        compiler_params=pltpu.CompilerParams(vmem_limit_bytes=40 * 2**20),
        cost_estimate=pl.CostEstimate(
            flops=4 * 2 * rows * 5 * TILE * HD, bytes_accessed=6 * 2**20, transcendentals=rows * 2560
        ),
        name="attend",
    )(count, ids, queries, keys, values, q_index, q_start, k_index, k_live)


def attend_back(
    count, ids, queries, keys, values, q_index, q_start, k_index, k_live, attended, d_out, lse, cosines, sines
):
    rows, span = queries.shape[0], keys.shape[0]
    tiles = span // TILE
    return pl.pallas_call(
        attend_back_kernel,
        grid_spec=pltpu.PrefetchScalarGridSpec(
            num_scalar_prefetch=2,
            grid=(rows // TILE,),
            in_specs=[
                by_query(2 * HD),
                whole((span, HD)),
                whole((span, HD)),
                by_query(1),
                by_query(1),
                whole((tiles, 1, TILE)),
                whole((tiles, 1, TILE)),
                by_query(2 * HD),
                by_query(2 * HD),
                by_query(2),
                by_query(HALF),
                by_query(HALF),
            ],
            out_specs=[by_query(2 * HD), whole((span, HD)), whole((span, HD))],
            scratch_shapes=[pltpu.VMEM((2 * TILE, HD), WIDE)],
        ),
        out_shape=[
            jax.ShapeDtypeStruct((rows, 2 * HD), LOW),
            jax.ShapeDtypeStruct((span, HD), WIDE),
            jax.ShapeDtypeStruct((span, HD), WIDE),
        ],
        compiler_params=pltpu.CompilerParams(vmem_limit_bytes=40 * 2**20),
        cost_estimate=pl.CostEstimate(
            flops=10 * 2 * rows * 5 * TILE * HD, bytes_accessed=12 * 2**20, transcendentals=rows * 2560
        ),
        name="attend_back",
    )(count, ids, queries, keys, values, q_index, q_start, k_index, k_live, attended, d_out, lse, cosines, sines)


def slot_order(array, x, c, y):
    for axis, bit in ((0, x), (1, c), (2, y)):
        array = jnp.where(bit == 1, jnp.flip(array, axis), array)
    moved = jnp.transpose(array, (1, 0, 2) + tuple(range(3, array.ndim)))
    return moved.reshape((8,) + array.shape[3:])


def o_rows_for_heads(o_proj, planes, x, c, y):
    if planes == 4:
        lines = lax.all_gather(o_proj, "r", axis=0).reshape((2, 2) + o_proj.shape)
        keep, send = pick(lines, y), pick(lines, 1 - y)
        received = across(send, "y", 1)
        low_half = jnp.where(y == 0, keep, received)
        high_half = jnp.where(y == 0, received, keep)
        return jnp.stack([low_half, high_half], axis=1).reshape(2 * HD, -1)
    full = lax.all_gather(o_proj, ALL, axis=0, tiled=True)
    heads = full.reshape(2, 2, 2, 2, HD, full.shape[1])
    return pick(pick(pick(heads, y), x, 1), c, 1).reshape(2 * HD, -1)


def o_grad_to_owner(grad, planes, r, x, c, y):
    width = grad.shape[1]
    if planes == 4:
        halves = grad.reshape(2, 2, HALF, width)
        keep = pick(halves, y, 1).astype(LOW)
        received = across(pick(halves, 1 - y, 1).astype(LOW), "y", 1)
        lines = jnp.concatenate(
            [jnp.where(y == 0, keep, received), jnp.where(y == 0, received, keep)], axis=0
        )
        return summed_over(lines, r, "r").astype(WIDE)
    place = jnp.zeros((2, 2, 2, 2, HD, width), WIDE)
    place = lax.dynamic_update_slice(
        place, grad.reshape(1, 2, 1, 1, HD, width), (y, 0, x, c, 0, 0)
    ).reshape(H * HD, width)
    return lax.psum_scatter(place, ALL, scatter_dimension=0, tiled=True)


def gains_to_owner(grads, r, x, c, y):
    kept = pick(grads, c, 2) + across(pick(grads, 1 - c, 2), "c", 1)
    kept = kept.reshape(kept.shape[0], 4, kept.shape[-1])
    place = x * 2 + y
    total = pick(kept, place, 1)
    for mask in range(1, 4):
        total = total + across(pick(kept, place ^ mask, 1), ("x", "y"), mask)
    result = pick(total, r)
    for mask in range(1, total.shape[0]):
        result = result + across(pick(total, r ^ mask), "r", mask)
    return result


def shards(
    inputs,
    out_grad,
    seq_lengths,
    key_live,
    attn_gain,
    q_down,
    q_gain,
    q_up,
    k_proj,
    v_proj,
    o_proj,
    ffn_gain,
    w_gate,
    w_up,
    w_down,
):
    rows, width = inputs.shape
    planes = lax.axis_size("r")
    r, x, c, y = (lax.axis_index(axis) for axis in ALL)
    place = x * 2 + y
    plane_rows = 8 * rows
    latent_width = q_down.shape[1]
    hidden_part = w_down.shape[0]
    hidden_width = 4 * hidden_part
    gate_rows = w_gate.shape[0]

    gains = lax.all_gather(jnp.concatenate([attn_gain, ffn_gain, q_gain]), ALL, axis=0).astype(WIDE)
    n_attn, n_ffn = attn_gain.shape[0], ffn_gain.shape[0]
    gain_attn = gains[:, :n_attn].reshape(1, -1)
    gain_ffn = gains[:, n_attn : n_attn + n_ffn].reshape(1, -1)
    gain_query = gains[:, n_attn + n_ffn :].reshape(1, -1)

    full_down = lax.all_gather(
        jnp.concatenate([q_down, k_proj, v_proj], axis=1), ALL, axis=0, tiled=True
    )

    up_rows = q_up.shape[0]
    q_up_sent = jnp.transpose(q_up.reshape(up_rows, 2, 2, 2, 2, HD), (3, 4, 1, 0, 2, 5))
    q_up_plane = lax.all_to_all(
        q_up_sent.reshape(8, up_rows, 2 * HD), PLANE, split_axis=0, concat_axis=0, tiled=True
    )
    q_up_heads = lax.all_gather(q_up_plane, "r", axis=0).reshape(latent_width, 2 * HD)
    o_heads = o_rows_for_heads(o_proj, planes, x, c, y)

    gate_up = jnp.stack([w_gate, w_up]).reshape(2, gate_rows, planes, 2, 2, 2, hidden_part)
    gate_up = jnp.transpose(gate_up, (0, 2, 4, 1, 3, 5, 6)).reshape(
        2, planes * 2, gate_rows, hidden_width
    )
    gate_up = lax.all_to_all(gate_up, ("r", "c"), split_axis=1, concat_axis=1, tiled=True)
    down_hidden = lax.all_gather(w_down, ("x", "y"), axis=0, tiled=True)
    gate_up = lax.all_gather(gate_up, ("x", "y"), axis=0)
    gate_up = jnp.transpose(
        gate_up.reshape(2, 2, 2, planes, 2, gate_rows, hidden_width), (2, 3, 0, 4, 1, 5, 6)
    ).reshape(2, width, hidden_width)
    gate_hidden, up_hidden = gate_up[0], gate_up[1]

    slots = jnp.arange(8, dtype=jnp.int32)
    slot_place = (
        ((slots // 2 % 2) ^ x) * 4 + ((slots // 4) ^ c) * 2 + ((slots % 2) ^ y)
    )
    within = slot_place[:, None] * rows + jnp.arange(rows, dtype=jnp.int32)[None, :]
    q_index = (r * plane_rows + within).reshape(plane_rows)
    q_start = token_tables(seq_lengths, q_index)
    cosines, sines = rope_tables(q_index - q_start)
    k_index = jnp.concatenate([q_index, q_index - plane_rows])
    live = jnp.concatenate([jnp.zeros((plane_rows,), jnp.int32), key_live])
    live = lax.dynamic_slice_in_dim(live, r * plane_rows, 2 * plane_rows)
    live = live.reshape(2, 2, 2, 2, rows)
    live = jnp.concatenate(
        [slot_order(live[1], x, c, y).reshape(-1), slot_order(live[0], x, c, y).reshape(-1)]
    )
    k_live = jnp.where(live == 1, k_index, -1)
    q_tiles, k_tiles = plane_rows // TILE, 2 * plane_rows // TILE
    q_tile, k_tile = q_index.reshape(q_tiles, TILE), k_index.reshape(k_tiles, TILE)
    needed = (
        jnp.max(k_tile, axis=1)[None, :] >= jnp.min(q_start.reshape(q_tiles, TILE), axis=1)[:, None]
    ) & (jnp.min(k_tile, axis=1)[None, :] <= jnp.max(q_tile, axis=1)[:, None])
    needed = needed.astype(jnp.int32)
    turn = jnp.cumsum(needed, axis=1) - 1
    chosen = (turn[:, None, :] == jnp.arange(k_tiles)[None, :, None]) & (needed[:, None, :] == 1)
    ids = jnp.sum(jnp.where(chosen, jnp.arange(k_tiles)[None, None, :], 0), axis=2)
    ids = ids.astype(jnp.int32).reshape(-1)
    count = jnp.sum(needed, axis=1).astype(jnp.int32)
    tables = (
        q_index[:, None],
        q_start[:, None],
        k_index.reshape(k_tiles, 1, TILE),
        k_live.reshape(k_tiles, 1, TILE),
    )

    out_grads = jnp.concatenate(gathered(out_grad, "r"), axis=0)

    x_float = inputs.astype(WIDE)
    normed_float, x_inv = norm_forward(x_float, gain_attn)
    normed = normed_float.astype(LOW)
    low = dot(normed, full_down, NN)
    latent = low[:, :latent_width]
    latent_float, latent_inv = norm_forward(latent, gain_query)
    key_rows = rotate(low[:, latent_width : latent_width + HD], cosines[:rows], sines[:rows])
    values = low[:, latent_width + HD :]
    own = jnp.concatenate([latent_float, key_rows, values], axis=1).astype(LOW)
    earlier = lax.ppermute(
        own[:, latent_width:], "r", [(source, source + 1) for source in range(planes - 1)]
    )
    plane = jnp.concatenate(gathered(jnp.concatenate([own, earlier], axis=1), ("x", "y")), axis=0)
    latents = plane[:, :latent_width]
    at = latent_width
    win_keys = jnp.concatenate([plane[:, at : at + HD], plane[:, at + 2 * HD : at + 3 * HD]])
    win_values = jnp.concatenate([plane[:, at + HD : at + 2 * HD], plane[:, at + 3 * HD :]])
    q_pre = dot(latents, q_up_heads, NN)
    queries = jnp.concatenate(
        [rotate(q_pre[:, :HD], cosines, sines), rotate(q_pre[:, HD:], cosines, sines)], axis=1
    ).astype(LOW)
    attended, log_total = attend(count, ids, queries, win_keys, win_values, *tables)
    o_mine = dot(attended[: plane_rows // 2], o_heads, NN).reshape(4, rows, width)
    o_partner = dot(attended[plane_rows // 2 :], o_heads, NN).astype(LOW).reshape(4, rows, width)
    middle = x_float + reduced(o_mine, o_partner, ("x", "y"))

    mid_float, mid_inv = norm_forward(middle, gain_ffn)
    normed_mid = jnp.concatenate(gathered(mid_float.astype(LOW), "r"), axis=0)
    gate_act = dot(normed_mid, gate_hidden, NN)
    up_act = dot(normed_mid, up_hidden, NN)
    sigmoid_gate = jax.nn.sigmoid(gate_act)
    silu_gate = gate_act * sigmoid_gate
    hidden = (silu_gate * up_act).astype(LOW)
    d_hidden = dot(out_grads, down_hidden, NT)
    d_gate = (d_hidden * up_act * sigmoid_gate * (1.0 + gate_act * (1.0 - sigmoid_gate))).astype(LOW)
    d_up = (d_hidden * silu_gate).astype(LOW)
    half = planes * rows

    def d_normed_of(part):
        return dot(d_gate[part], gate_hidden, NT) + dot(d_up[part], up_hidden, NT)

    d_partner = d_normed_of(slice(half, None)).astype(LOW).reshape(planes, rows, width)
    d_mine = d_normed_of(slice(0, half)).reshape(planes, rows, width)
    d_normed_mid = reduced(d_mine, d_partner, "r")
    out_partner = dot(hidden[half:], down_hidden, NN).astype(LOW).reshape(planes, rows, width)
    out_mine = dot(hidden[:half], down_hidden, NN).reshape(planes, rows, width)
    output = (middle + reduced(out_mine, out_partner, "r")).astype(LOW)
    grad_down = dot(hidden, out_grads, TN).reshape(4, hidden_part, width)
    grad_down = summed_over(grad_down, place, ("x", "y"))

    def rows_by_place(grad):
        grad = grad.reshape(planes, 2, 2, 2, gate_rows, hidden_width)
        return jnp.transpose(grad, (1, 3, 0, 2, 4, 5)).reshape(
            4, planes * 2, gate_rows, hidden_width
        )

    grad_gate_up = jnp.stack(
        [
            rows_by_place(dot(normed_mid, d_gate, TN)),
            rows_by_place(dot(normed_mid, d_up, TN)),
        ],
        axis=1,
    )
    grad_gate_up = summed_over(grad_gate_up, place, ("x", "y")).astype(LOW)
    grad_gate_up = lax.all_to_all(grad_gate_up, ("r", "c"), split_axis=1, concat_axis=1, tiled=True)
    grad_gate_up = jnp.transpose(
        grad_gate_up.reshape(2, planes, 2, gate_rows, 2, 2, hidden_part), (0, 3, 1, 4, 2, 5, 6)
    ).reshape(2, gate_rows, -1)
    grad_gate_up = grad_gate_up.astype(WIDE)

    d_mid_norm, grad_gain_ffn = norm_backward(middle, mid_inv, gain_ffn, d_normed_mid)
    d_middle = out_grad.astype(WIDE) + d_mid_norm
    d_middles = jnp.concatenate(gathered(d_middle.astype(LOW), ("x", "y")), axis=0)
    d_attended = dot(d_middles, o_heads, NT).astype(LOW)
    grad_o = o_grad_to_owner(dot(attended, d_middles, TN), planes, r, x, c, y)
    dq_low, d_win_keys, d_win_values = attend_back(
        count,
        ids,
        queries,
        win_keys,
        win_values,
        *tables,
        attended,
        d_attended,
        log_total,
        cosines,
        sines,
    )
    d_latents = dot(dq_low, q_up_heads, NT)
    terms = jnp.concatenate(
        [
            d_latents,
            d_win_keys[:plane_rows],
            d_win_values[:plane_rows],
            d_win_keys[plane_rows:],
            d_win_values[plane_rows:],
        ],
        axis=1,
    ).reshape(2, 4, rows, -1)
    summed = reduced(terms[0], terms[1].astype(LOW), ("x", "y"))
    later = lax.ppermute(
        summed[:, latent_width + 2 * HD :].astype(LOW),
        "r",
        [(source, source - 1) for source in range(1, planes)],
    ).astype(WIDE)
    own_grads = summed[:, latent_width : latent_width + 2 * HD] + later
    dk_low = rotate(own_grads[:, :HD], cosines[:rows], -sines[:rows]).astype(LOW)
    dv_low = own_grads[:, HD:].astype(LOW)
    grad_q_up = dot(latents, dq_low, TN).reshape(planes, 8, up_rows, 2 * HD)
    grad_q_up = summed_over(grad_q_up, r, "r").astype(LOW)
    grad_q_up = lax.all_to_all(grad_q_up, PLANE, split_axis=0, concat_axis=0, tiled=True)
    grad_q_up = jnp.transpose(
        grad_q_up.reshape(2, 2, 2, up_rows, 2, HD), (3, 2, 4, 0, 1, 5)
    ).reshape(up_rows, -1)
    grad_q_up = grad_q_up.astype(WIDE)

    d_latent, grad_gain_query = norm_backward(
        latent, latent_inv, gain_query, summed[:, :latent_width]
    )
    d_low = jnp.concatenate([d_latent.astype(LOW), dk_low, dv_low], axis=1)
    d_lows = lax.all_gather(d_low, PLANE, axis=0, tiled=True)
    columns = jnp.transpose(
        normed.reshape(rows, planes, 8, gate_rows), (2, 0, 1, 3)
    ).reshape(8, rows, planes * gate_rows)
    columns = lax.all_to_all(columns, PLANE, split_axis=0, concat_axis=0, tiled=True)
    grad_low = dot(columns.reshape(plane_rows, -1), d_lows, TN).reshape(planes, gate_rows, -1)
    grad_low = summed_over(grad_low, r, "r")
    d_normed = dot(d_low, full_down, NT)
    d_x_norm, grad_gain_attn = norm_backward(x_float, x_inv, gain_attn, d_normed)
    input_grad = d_middle + d_x_norm
    grad_gains = jnp.concatenate(
        [
            grad_gain_attn.reshape(planes, 2, 2, 2, -1),
            grad_gain_ffn.reshape(planes, 2, 2, 2, -1),
            grad_gain_query.reshape(planes, 2, 2, 2, -1),
        ],
        axis=-1,
    )
    grad_gains = gains_to_owner(grad_gains, r, x, c, y)
    return (
        output,
        input_grad,
        grad_gains[:n_attn],
        grad_low[:, :latent_width],
        grad_gains[n_attn + n_ffn :],
        grad_q_up,
        grad_low[:, latent_width : latent_width + HD],
        grad_low[:, latent_width + HD :],
        grad_o,
        grad_gains[n_attn : n_attn + n_ffn],
        grad_gate_up[0],
        grad_gate_up[1],
        grad_down,
    )


def solution(mesh):
    devices = mesh.devices.reshape(-1, 2, 2, 2)
    grid = Mesh(devices, ALL)
    split, split_rows = P(ALL), P(ALL, None)
    placed = (split_rows, split_rows, P(), P(), split, split_rows, split) + (split_rows,) * 4 + (
        split,
    ) + (split_rows,) * 3
    return jax.shard_map(
        shards,
        mesh=grid,
        in_specs=placed,
        out_specs=(
            (split_rows, split_rows, split, split_rows, split)
            + (split_rows,) * 4
            + (split,)
            + (split_rows,) * 3
        ),
        check_vma=False,
    )
```
